512 devices in a mesh: grp: 16 (over z, core), blk: 32 (over x, y).
Axes of the slice: x: 4, y: 8, z: 8, core: 2. Of those that a mesh axis runs over, the one named last changes fastest.
Arguments:
- leaf_blocks: float32 [16, 256, 256], P('grp'), may hold values from 0 to 5, as said below
- leaf_rhs: float32 [16, 256, 8192], P('grp', None, 'blk'), may hold values from -0.24 to 0.24
- bases: bfloat16 [16, 512, 512], P('grp'), may hold values from -1 to 2, as said below
- couplings: bfloat16 [16, 256, 256], P('grp'), may hold values from -1 to 1, as said below
Outputs:
- root_solution: float32 [256, 8192], P('grp', 'blk')
The draws below stay inside these ranges and needn't reach their ends.
Inputs may be any that keep to these rules, and one draw needn't show every extreme that they name: `leaf_blocks`: each block is symmetric, and every merged matrix and Schur complement of the levels is positive definite. `bases`: each transform is nonsingular; slot 0 is not an owner. `couplings`: slot 0 is not an owner.
All inputs are finite; a program needn't handle non-finite values.
Results may differ from the reference program's by a relative error of at most 0.0003.
Values may be sent and summed in bfloat16 or wider, within the bound.
A program may use at most 64 MiB of HBM per device.

```python
import math
import jax
import jax.numpy as jnp
from jax import lax

R = 256
NODES = 16
RHS = 8192


def draw_leaf_blocks(key, part):
    key = jax.random.fold_in(key, 11)
    key_pos, key_side, key_scale, key_floor = jax.random.split(key, 4)
    reach = 33.0
    side_reach = 0.5
    scale_lo, scale_hi = (0.6, 1.6)
    floor_lo, floor_hi = (0.02, 0.05)
    jitter = jax.random.uniform(key_pos, (NODES, R), jnp.float32, 0.0, 0.4)
    cells = jnp.arange(R, dtype=jnp.float32)[None, :] + jitter
    lateral = jax.random.uniform(key_side, (NODES, R), jnp.float32)
    scales = jnp.exp(jax.random.uniform(key_scale, (NODES, R), jnp.float32, math.log(scale_lo), math.log(scale_hi)))
    floors = jnp.exp(jax.random.uniform(key_floor, (NODES, R), jnp.float32, math.log(floor_lo), math.log(floor_hi)))
    distance = jnp.abs(cells[:, :, None] - cells[:, None, :]) / reach + jnp.abs(lateral[:, :, None] - lateral[:, None, :]) / side_reach
    kernel = jnp.exp(-distance) * scales[:, :, None] * scales[:, None, :]
    eye = (jnp.arange(R)[:, None] == jnp.arange(R)[None, :]).astype(jnp.float32)
    return kernel + eye[None, :, :] * floors[:, :, None]


def draw_bases(key, part):
    key = jax.random.fold_in(key, 23)
    scale = 0.15 / (2 * R) ** 0.5
    extra = jax.random.truncated_normal(key, -4.0, 4.0, (NODES, 2 * R, 2 * R), jnp.float32) * scale
    eye = (jnp.arange(2 * R)[:, None] == jnp.arange(2 * R)[None, :]).astype(jnp.float32)
    return (eye[None, :, :] + extra).astype(jnp.bfloat16)


def draw_couplings(key, part):
    key = jax.random.fold_in(key, 37)
    scale = 0.004 / R ** 0.5
    values = jax.random.truncated_normal(key, -4.0, 4.0, (NODES, R, R), jnp.float32) * scale
    return values.astype(jnp.bfloat16)


def block_scale(stream_key, shape, shards, smallest, largest):
    loudness, own = 1.0, jax.random.fold_in(stream_key, 6)
    for position, shards_of in shards:
        heights = jnp.exp(jax.random.uniform(jax.random.fold_in(own, position), (shards_of,), jnp.float32, smallest / len(shards), largest / len(shards)))
        loudness = loudness * jnp.repeat(heights, shape[position] // shards_of).reshape([-1 if axis == position else 1 for axis in range(len(shape))])
    return loudness


def gaussian(own_key, extent, deviation, most, cuts=(), held_as=jnp.bfloat16):
    array = jax.random.normal(own_key, extent, jnp.float32) * deviation
    if len(cuts) > 0:
        array = block_scale(own_key, extent, cuts, -0.22, 0.18) * array
    return jnp.clip(array, min=-most, max=most).astype(held_as)


def setup_inputs(seed: int = 0) -> dict:
    keys = jax.random.split(jax.random.key(seed), 5)
    leaf_blocks = draw_leaf_blocks(jax.random.fold_in(keys[4], 71), 0)
    leaf_rhs = gaussian(keys[1], (NODES, R, RHS), 0.04, 0.24, ((0, 16), (2, 32)), jnp.float32)
    bases = draw_bases(jax.random.fold_in(keys[4], 71), 0)
    couplings = draw_couplings(jax.random.fold_in(keys[4], 71), 0)
    return {"leaf_blocks": leaf_blocks, "leaf_rhs": leaf_rhs, "bases": bases, "couplings": couplings}


def merge(first, second, first_rhs, second_rhs, base, coupling):
    high = lax.Precision.HIGHEST
    rank = first.shape[0]
    transform = base.astype(jnp.float32)
    link = coupling.astype(jnp.float32)
    merged = jnp.concatenate([jnp.concatenate([first, link], 1), jnp.concatenate([link.T, second], 1)], 0)
    coupled = jnp.dot(transform.T, jnp.dot(merged, transform, precision=high), precision=high)
    lower = jnp.linalg.cholesky(coupled[:rank, :rank])
    factor = jax.scipy.linalg.solve_triangular(lower, coupled[:rank, rank:], lower=True)
    block = coupled[rank:, rank:] - jnp.dot(factor.T, factor, precision=high)
    mixed = jnp.dot(transform.T, jnp.concatenate([first_rhs, second_rhs], 0), precision=high)
    solved = jax.scipy.linalg.solve_triangular(lower, mixed[:rank], lower=True)
    rhs_next = mixed[rank:] - jnp.dot(factor.T, solved, precision=high)
    return (block, rhs_next)

def reference(leaf_blocks, leaf_rhs, bases, couplings):
    blocks = [leaf_blocks[i] for i in range(NODES)]
    sides = [leaf_rhs[i] for i in range(NODES)]
    levels = NODES.bit_length() - 1
    for level in range(levels):
        new_blocks = []
        new_sides = []
        for parent in range(len(blocks) // 2):
            owner = parent * (2 << level) + (1 << level)
            block, side = merge(blocks[2 * parent], blocks[2 * parent + 1], sides[2 * parent], sides[2 * parent + 1], bases[owner], couplings[owner])
            new_blocks.append(block)
            new_sides.append(side)
        blocks = new_blocks
        sides = new_sides
    lower = jnp.linalg.cholesky(blocks[0])
    return jax.scipy.linalg.cho_solve((lower, True), sides[0])
```

```python
import functools
import jax
import jax.numpy as jnp
from jax import lax
from jax.experimental import pallas as pl
from jax.experimental.pallas import tpu as pltpu
from jax.sharding import PartitionSpec as P

F32 = jnp.float32
BF16 = jnp.bfloat16
HIGH = lax.Precision.HIGHEST
LANES = 128
WIDE = 16


def reciprocal(x):
    return pl.reciprocal(x, approx=True)


def dot(a, b):
    return jnp.dot(a, b, preferred_element_type=F32)


def dot_full(a, b):
    return jnp.dot(a, b, preferred_element_type=F32, precision=HIGH)


def dot_full_t(a, b):
    return lax.dot_general(a, b, (((0,), (0,)), ((), ())), preferred_element_type=F32, precision=HIGH)


def pieces(x, count):
    out = []
    for _ in range(count - 1):
        part = x.astype(BF16)
        out.append(part)
        x = x - part.astype(F32)
    out.append(x.astype(BF16))
    return out


def eliminate(tile, size):
    tiles = WIDE // 8
    rows = tile.reshape(size // 8, 8, LANES)
    sub = lax.broadcasted_iota(jnp.int32, (8, LANES), 0)
    outs = []

    def spread(x, c):
        return jnp.broadcast_to(x[c : c + 1, :], (8, LANES))

    for start in range(0, size, WIDE):
        m = (size - start) // 8
        cols = [jnp.broadcast_to(rows[:, :, start + c : start + c + 1], (m, 8, LANES)) for c in range(WIDE)]
        pivots = [jnp.ones((8, LANES), F32) for _ in range(tiles)]
        for c in range(WIDE):
            q, cc = c // 8, c % 8
            pivot = spread(cols[c][q], cc)
            inverse = reciprocal(pivot)
            pivots[q] = jnp.where(sub == cc, pivot, pivots[q])
            head = jnp.where(sub > cc, cols[c][q], 0.0)[None]
            below = jnp.concatenate([head, cols[c][q + 1 :]], 0) if q + 1 < m else head
            for d in range(c + 1, WIDE):
                new = cols[d][q:] - below * (spread(cols[d][q], cc) * inverse)[None]
                cols[d] = jnp.concatenate([cols[d][:q], new], 0) if q else new
            new = rows[q:] - below * (spread(rows[q], cc) * inverse)[None]
            rows = jnp.concatenate([rows[:q], new], 0) if q else new
        for q in range(tiles):
            outs.append(rows[q] * lax.rsqrt(pivots[q]))
        rows = rows[tiles:]
    return jnp.concatenate(outs, 0)


def inverse_factor(a_ref, out_ref):
    h = LANES // 2
    eye = jnp.where(
        lax.broadcasted_iota(jnp.int32, (h, h), 0) == lax.broadcasted_iota(jnp.int32, (h, h), 1), 1.0, 0.0
    ).astype(F32)
    first = eliminate(jnp.concatenate([a_ref[:h, :h], eye], 1), h)[:, h:]
    reach = dot_full(first, a_ref[:h, h:])
    rest = a_ref[h:, h:] - dot_full_t(reach, reach)
    second = eliminate(jnp.concatenate([rest, eye], 1), h)[:, h:]
    corner = -dot_full(second, dot_full_t(reach, first))
    out_ref[:h, :] = jnp.concatenate([first, jnp.zeros((h, h), F32)], 1)
    out_ref[h:, :] = jnp.concatenate([corner, second], 1)


def kernel(
    groups, levels, rank, leaf_s, leaf_y, base, link, out,
    s_own, s_got, y_own, y_got, w_all, b_all, mix, upper, akk, linv, reach, vee, xs,
    local_sem, s_send, s_recv, y_send, y_recv, w_send, w_recv, b_send, b_recv,
):
    me = lax.axis_index("grp")
    half = rank // 2

    def local_id(level):
        return lax.rem(me, 2 << level)

    def is_first(level):
        return lax.rem(me // (1 << level), 2) == 0

    def partner(level):
        return jnp.where(is_first(level), me + (1 << level), me - (1 << level))

    def owner(level):
        return local_id(level) == 1 << level

    def sends(level, bit):
        if bit == level:
            return owner(level)
        return lax.rem(local_id(level), 2 << bit) == 0

    def gets(level, bit):
        if bit == level:
            return local_id(level) == 0
        return lax.rem(local_id(level), 2 << bit) == 1 << bit

    def remote(src, dst, send, recv, bit):
        return pltpu.make_async_remote_copy(
            src_ref=src, dst_ref=dst, send_sem=send, recv_sem=recv,
            device_id={"grp": partner(bit)}, device_id_type=pl.DeviceIdType.MESH,
        )

    def base_copies(level, bit):
        here = bit == level
        return (
            remote(base.at[0] if here else w_all.at[level], w_all.at[level], w_send.at[level, bit], w_recv.at[level], bit),
            remote(link.at[0] if here else b_all.at[level], b_all.at[level], b_send.at[level, bit], b_recv.at[level], bit),
        )

    def s_copy(level):
        return remote(leaf_s.at[0] if level == 0 else s_own.at[level], s_got.at[level], s_send.at[level], s_recv.at[level], level)

    def y_copy(level):
        return remote(leaf_y.at[0] if level == 0 else y_own.at[level], y_got.at[level], y_send.at[level], y_recv.at[level], level)

    def start_bases(level, bit):
        @pl.when(sends(level, bit))
        def _():
            for copy in base_copies(level, bit):
                copy.start()

    def await_bases(level, bit):
        @pl.when(gets(level, bit))
        def _():
            for copy in base_copies(level, bit):
                copy.wait_recv()

    def own_copies(level):
        return (
            pltpu.make_async_copy(base.at[0], w_all.at[level], local_sem.at[2]),
            pltpu.make_async_copy(link.at[0], b_all.at[level], local_sem.at[3]),
        )

    leaf_copies = (
        pltpu.make_async_copy(leaf_s.at[0], s_own.at[0], local_sem.at[0]),
        pltpu.make_async_copy(leaf_y.at[0], y_own.at[0], local_sem.at[1]),
    )
    for copy in leaf_copies:
        copy.start()
    for level in range(levels):
        @pl.when(owner(level))
        def _():
            for copy in own_copies(level):
                copy.start()

    barrier = pltpu.get_barrier_semaphore()
    for level in range(levels):
        pl.semaphore_signal(barrier, inc=1, device_id={"grp": partner(level)}, device_id_type=pl.DeviceIdType.MESH)
    pl.semaphore_wait(barrier, levels)

    start_bases(0, 0)
    s_copy(0).start()
    for level in range(1, levels):
        start_bases(level, level)
    y_copy(0).start()

    for copy in leaf_copies:
        copy.wait()
    for level in range(levels):
        @pl.when(owner(level))
        def _():
            for copy in own_copies(level):
                copy.wait()

    def step(i, carry):
        level, part = i // 2, lax.rem(i, 2)

        @pl.when(part == 0)
        def _():
            for known in range(levels):
                @pl.when(level == known)
                def _():
                    await_bases(known, 0)
                    s_copy(known).wait_recv()

            @pl.when(level < levels)
            def _():
                first = lax.rem(me // jnp.where(level == 0, 1, jnp.where(level == 1, 2, jnp.where(level == 2, 4, 8))), 2) == 0
                mine, other = s_own[level], s_got[level]
                w_top, w_low, b = w_all[level, :rank, :], w_all[level, rank:, :], b_all[level]
                for at, own, cross in ((0, w_top, dot(b, w_low)),
                                       (rank, w_low, lax.dot_general(b, w_top, (((0,), (0,)), ((), ())), preferred_element_type=F32))):
                    block = jnp.where(first, mine, other) if at == 0 else jnp.where(first, other, mine)
                    hi, mid, low = pieces(block, 3)
                    mix[at : at + rank, :] = dot(low, own) + dot(mid, own) + cross + dot(hi, own)
                hi, mid, low = pieces(mix[...], 3)
                w_t = w_all[level].T
                upper[...] = dot(w_t, low) + dot(w_t, mid) + dot(w_t, hi)

            @pl.when(level == levels)
            def _():
                upper[:rank, :rank] = s_own[levels]

            akk[...] = upper[:half, :half]

        inverse_factor(akk, linv.at[part])

        @pl.when(part == 0)
        def _():
            reach[...] = dot_full(linv[0], upper[:half, half:])
            rest = upper[half:rank, half:] - dot_full_t(reach[:, :half], reach[...])
            akk[...] = rest[:, :half]
            vee[:half, :] = reach[:, half:]
            vee[half:, :] = rest[:, half:]

        @pl.when(part == 1)
        def _():
            @pl.when(level < levels)
            def _():
                vee[half:, :] = dot_full(linv[1], vee[half:, :])
                s_own[level + 1] = upper[rank:, rank:] - dot_full_t(vee[...], vee[...])
                for known in range(levels):
                    @pl.when(level == known)
                    def _():
                        if known + 1 < levels:
                            s_copy(known + 1).start()
                        y_copy(known).wait_recv()
                        for later in range(known + 1, levels):
                            bit = later - known - 1
                            await_bases(later, bit + 1)
                            start_bases(later, bit)
                first = lax.rem(me // jnp.where(level == 0, 1, jnp.where(level == 1, 2, jnp.where(level == 2, 4, 8))), 2) == 0
                mine, other = y_own[level], y_got[level]
                mixed = jnp.zeros((2 * rank, mine.shape[1]), F32)
                w_t = w_all[level].T
                for at in (0, rank):
                    block = jnp.where(first, mine, other) if at == 0 else jnp.where(first, other, mine)
                    hi, mid, low = pieces(block, 3)
                    cut = w_t[:, at : at + rank]
                    mixed = mixed + (dot(cut, low) + dot(cut, mid) + dot(cut, hi))
                top = dot_full(linv[0], mixed[:half])
                low = dot_full(linv[1], mixed[half:rank] - dot_full_t(reach[:, :half], top))
                y_own[level + 1] = mixed[rank:] - dot_full_t(vee[...], jnp.concatenate([top, low], 0))
                for known in range(levels - 1):
                    @pl.when(level == known)
                    def _():
                        y_copy(known + 1).start()

            @pl.when(level == levels)
            def _():
                top = dot_full(linv[0], y_own[levels, :half])
                low = dot_full(linv[1], y_own[levels, half:] - dot_full_t(reach[:, :half], top))
                low = dot_full_t(linv[1], low)
                xs[half:, :] = low
                xs[:half, :] = dot_full_t(linv[0], top - dot_full(reach[:, :half], low))

        return carry

    lax.fori_loop(0, 2 * levels + 2, step, 0)

    share = rank // groups
    out[...] = xs[pl.ds(pl.multiple_of(me * share, share), share), :]

    for level in range(levels):
        s_copy(level).wait_send()
        y_copy(level).wait_send()
        for bit in range(level + 1):
            @pl.when(sends(level, bit))
            def _():
                for copy in base_copies(level, bit):
                    copy.wait_send()


def body(leaf_blocks, leaf_rhs, bases, couplings):
    groups = lax.axis_size("grp")
    levels = groups.bit_length() - 1
    rank = leaf_blocks.shape[1]
    width = leaf_rhs.shape[2]
    any_space = pl.BlockSpec(memory_space=pl.ANY)
    return pl.pallas_call(
        functools.partial(kernel, groups, levels, rank),
        out_shape=jax.ShapeDtypeStruct((rank // groups, width), F32),
        in_specs=[any_space] * 4,
        out_specs=pl.BlockSpec(memory_space=pltpu.VMEM),
        scratch_shapes=[
            pltpu.VMEM((levels + 1, rank, rank), F32),
            pltpu.VMEM((levels, rank, rank), F32),
            pltpu.VMEM((levels + 1, rank, width), F32),
            pltpu.VMEM((levels, rank, width), F32),
            pltpu.VMEM((levels, 2 * rank, 2 * rank), BF16),
            pltpu.VMEM((levels, rank, rank), BF16),
            pltpu.VMEM((2 * rank, 2 * rank), F32),
            pltpu.VMEM((2 * rank, 2 * rank), F32),
            pltpu.VMEM((rank // 2, rank // 2), F32),
            pltpu.VMEM((2, rank // 2, rank // 2), F32),
            pltpu.VMEM((rank // 2, 3 * rank // 2), F32),
            pltpu.VMEM((rank, rank), F32),
            pltpu.VMEM((rank, width), F32),
            pltpu.SemaphoreType.DMA((4,)),
            pltpu.SemaphoreType.DMA((levels,)),
            pltpu.SemaphoreType.DMA((levels,)),
            pltpu.SemaphoreType.DMA((levels,)),
            pltpu.SemaphoreType.DMA((levels,)),
            pltpu.SemaphoreType.DMA((levels, levels)),
            pltpu.SemaphoreType.DMA((levels,)),
            pltpu.SemaphoreType.DMA((levels, levels)),
            pltpu.SemaphoreType.DMA((levels,)),
        ],
        compiler_params=pltpu.CompilerParams(
            collective_id=0, has_side_effects=True, vmem_limit_bytes=48 << 20
        ),
    )(leaf_blocks, leaf_rhs, bases, couplings)


def solution(mesh):
    placed = (
        P("grp", None, None),
        P("grp", None, "blk"),
        P("grp", None, None),
        P("grp", None, None),
    )
    return jax.shard_map(
        body, mesh=mesh, in_specs=placed, out_specs=P("grp", "blk"), check_vma=False
    )
```

```python
import functools
import jax
import jax.numpy as jnp
from jax import lax
from jax.experimental import pallas as pl
from jax.experimental.pallas import tpu as pltpu
from jax.sharding import PartitionSpec as P

F32 = jnp.float32
BF16 = jnp.bfloat16
HIGH = lax.Precision.HIGHEST
LANES = 128
WIDE = 16


def reciprocal(x):
    return pl.reciprocal(x, approx=True)


def dot(a, b):
    return jnp.dot(a, b, preferred_element_type=F32)


def dot_full(a, b):
    return jnp.dot(a, b, preferred_element_type=F32, precision=HIGH)


def dot_full_t(a, b):
    return lax.dot_general(a, b, (((0,), (0,)), ((), ())), preferred_element_type=F32, precision=HIGH)


def pieces(x, count):
    out = []
    for _ in range(count - 1):
        part = x.astype(BF16)
        out.append(part)
        x = x - part.astype(F32)
    out.append(x.astype(BF16))
    return out


def eliminate(tile, size):
    tiles = WIDE // 8
    rows = tile.reshape(size // 8, 8, LANES)
    sub = lax.broadcasted_iota(jnp.int32, (8, LANES), 0)
    outs = []

    def spread(x, c):
        return jnp.broadcast_to(x[c : c + 1, :], (8, LANES))

    for start in range(0, size, WIDE):
        m = (size - start) // 8
        cols = [jnp.broadcast_to(rows[:, :, start + c : start + c + 1], (m, 8, LANES)) for c in range(WIDE)]
        pivots = [jnp.ones((8, LANES), F32) for _ in range(tiles)]
        for c in range(WIDE):
            q, cc = c // 8, c % 8
            pivot = spread(cols[c][q], cc)
            inverse = reciprocal(pivot)
            pivots[q] = jnp.where(sub == cc, pivot, pivots[q])
            head = jnp.where(sub > cc, cols[c][q], 0.0)[None]
            below = jnp.concatenate([head, cols[c][q + 1 :]], 0) if q + 1 < m else head
            for d in range(c + 1, WIDE):
                new = cols[d][q:] - below * (spread(cols[d][q], cc) * inverse)[None]
                cols[d] = jnp.concatenate([cols[d][:q], new], 0) if q else new
            new = rows[q:] - below * (spread(rows[q], cc) * inverse)[None]
            rows = jnp.concatenate([rows[:q], new], 0) if q else new
        for q in range(tiles):
            outs.append(rows[q] * lax.rsqrt(pivots[q]))
        rows = rows[tiles:]
    return jnp.concatenate(outs, 0)


def inverse_factor(a_ref, out_ref):
    h = LANES // 2
    eye = jnp.where(
        lax.broadcasted_iota(jnp.int32, (h, h), 0) == lax.broadcasted_iota(jnp.int32, (h, h), 1), 1.0, 0.0
    ).astype(F32)
    first = eliminate(jnp.concatenate([a_ref[:h, :h], eye], 1), h)[:, h:]
    reach = dot_full(first, a_ref[:h, h:])
    rest = a_ref[h:, h:] - dot_full_t(reach, reach)
    second = eliminate(jnp.concatenate([rest, eye], 1), h)[:, h:]
    corner = -dot_full(second, dot_full_t(reach, first))
    out_ref[:h, :] = jnp.concatenate([first, jnp.zeros((h, h), F32)], 1)
    out_ref[h:, :] = jnp.concatenate([corner, second], 1)


def kernel(
    groups, rank, leaf_s, leaf_y, base, link, out,
    s_in, y_in, w, w_t, b, mix, cross, upper, akk, linv, reach, vee, s_out, y_out, xs, rows_in,
    local_sem, s_send, s_recv, y_send, y_recv, leaf_send, x_send, x_recv,
):
    me = lax.axis_index("grp")
    half = rank // 2
    root = groups // 2
    share = rank // groups
    odd = lax.rem(me, 2) == 1
    step = jnp.int32(1)
    bits = groups.bit_length() - 1
    for bit in range(bits):
        step = jnp.where(lax.rem(me, 2 << bit) == 1 << bit, 1 << bit, step)
    second = lax.rem(me // (2 * step), 2)
    target = me + step - 2 * step * second

    def remote(src, dst, send, recv, group):
        return pltpu.make_async_remote_copy(
            src_ref=src, dst_ref=dst, send_sem=send, recv_sem=recv,
            device_id={"grp": group}, device_id_type=pl.DeviceIdType.MESH,
        )

    cuts = ((pl.ds(0, half), pl.ds(0, rank)), (pl.ds(half, half), pl.ds(half, half)))

    def s_copies(src, sems, slot, group):
        return [
            remote(src.at[cut], s_in.at[(slot, *cut)], sems.at[k], s_recv.at[slot, k], group)
            for k, cut in enumerate(cuts)
        ]

    leaf_s_copies = s_copies(leaf_s.at[0], leaf_send, 0, me + 1)
    leaf_y_copy = remote(leaf_y.at[0], y_in.at[0], leaf_send.at[2], y_recv.at[0], me + 1)
    up_s_copies = s_copies(s_out, s_send, second, target)
    up_y_copy = remote(y_out, y_in.at[second], y_send, y_recv.at[second], target)
    own_s = pltpu.make_async_copy(leaf_s.at[0], s_in.at[1], local_sem.at[0])
    own_y = pltpu.make_async_copy(leaf_y.at[0], y_in.at[1], local_sem.at[1])
    own_w = pltpu.make_async_copy(base.at[0], w, local_sem.at[2])
    own_b = pltpu.make_async_copy(link.at[0], b, local_sem.at[3])

    barrier = pltpu.get_barrier_semaphore()

    def greet(group):
        pl.semaphore_signal(barrier, inc=1, device_id={"grp": group}, device_id_type=pl.DeviceIdType.MESH)

    @pl.when(odd)
    def _():
        greet(me - 1)
        own_s.start()

    for bit in range(1, bits):
        @pl.when(lax.rem(me, 2 << bit) == 1 << bit)
        def _():
            lean = 0 if bit == 1 else 1
            greet(me - (1 << bit) // 2 + lean)
            greet(me + (1 << bit) // 2 + lean)

    @pl.when(jnp.logical_not(odd))
    def _():
        pl.semaphore_wait(barrier, 1)
        for copy in leaf_s_copies:
            copy.start()
        leaf_y_copy.start()

    own_w.start()
    own_b.start()

    @pl.when(odd)
    def _():
        own_y.start()

    own_w.wait()
    own_b.wait()

    def factor():
        def turn(part, carry):
            inverse_factor(akk, linv.at[part])

            @pl.when(part == 0)
            def _():
                reach[...] = dot_full(linv[0], upper[:half, half:])
                rest = upper[half:rank, half:] - dot_full_t(reach[:, :half], reach[...])
                akk[...] = rest[:, :half]
                vee[:half, :] = reach[:, half:]
                vee[half:, :] = rest[:, half:]

            return carry

        lax.fori_loop(0, 2, turn, 0)

    @pl.when(me > 0)
    def _():
        w_t[...] = w[...].T
        cross[:rank, :] = dot(b[...], w[rank:, :])
        cross[rank:, :] = lax.dot_general(b[...], w[:rank, :], (((0,), (0,)), ((), ())), preferred_element_type=F32)
        for copy in s_copies(s_out, s_send, 0, target):
            copy.wait_recv()

        @pl.when(odd)
        def _():
            own_s.wait()

        @pl.when(jnp.logical_not(odd))
        def _():
            for copy in s_copies(s_out, s_send, 1, target):
                copy.wait_recv()

        for slot in (0, 1):
            at = slot * rank
            s_in[slot, half:, :half] = s_in[slot, :half, half:].T
            hi, mid, low = pieces(s_in[slot], 3)
            own = w[at : at + rank, :]
            mix[at : at + rank, :] = dot(low, own) + dot(mid, own) + cross[at : at + rank, :] + dot(hi, own)
        hi, mid, low = pieces(mix[...], 3)
        upper[:rank, :] = dot(w_t[:rank, :], low) + dot(w_t[:rank, :], mid) + dot(w_t[:rank, :], hi)
        lower = w_t[rank:, :]
        upper[rank:, rank:] = dot(lower, low[:, rank:]) + dot(lower, mid[:, rank:]) + dot(lower, hi[:, rank:])
        akk[...] = upper[:half, :half]
        factor()
        vee[half:, :] = dot_full(linv[1], vee[half:, :])

        @pl.when(odd)
        def _():
            extra = lax.rem(me, 4) == 3
            for bit in range(3, bits):
                for sign in (-1, 1):
                    for owner in range(1 << bit, groups, 2 << bit):
                        extra = extra | (me == owner + sign * (1 << bit) // 2 + 1)
            pl.semaphore_wait(barrier, jnp.where(extra, 2, 1))

        s_out[:half, :] = upper[rank : rank + half, rank:] - dot_full_t(vee[:, :half], vee[...])

        @pl.when(me != root)
        def _():
            up_s_copies[0].start()

        s_out[half:, half:] = upper[rank + half :, rank + half :] - dot_full_t(vee[:, half:], vee[:, half:])

        @pl.when(me != root)
        def _():
            up_s_copies[1].start()

        remote(y_out, y_in.at[0], y_send, y_recv.at[0], target).wait_recv()

        @pl.when(odd)
        def _():
            own_y.wait()

        @pl.when(jnp.logical_not(odd))
        def _():
            remote(y_out, y_in.at[1], y_send, y_recv.at[1], target).wait_recv()

        mixed = jnp.zeros((2 * rank, y_in.shape[2]), F32)
        for slot in (0, 1):
            hi, mid, low = pieces(y_in[slot], 3)
            cut = w_t[:, slot * rank : (slot + 1) * rank]
            mixed = mixed + (dot(cut, low) + dot(cut, mid) + dot(cut, hi))
        top = dot_full(linv[0], mixed[:half])
        low = dot_full(linv[1], mixed[half:rank] - dot_full_t(reach[:, :half], top))
        y_out[...] = mixed[rank:] - dot_full_t(vee[...], jnp.concatenate([top, low], 0))

        @pl.when(me != root)
        def _():
            up_y_copy.start()

    def x_copy(group):
        return remote(xs.at[pl.ds(group * share, share), :], rows_in, x_send.at[group], x_recv, group)

    @pl.when(me == root)
    def _():
        s_out[half:, :half] = s_out[:half, half:].T
        upper[:rank, :rank] = s_out[...]
        akk[...] = s_out[:half, :half]
        factor()
        top = dot_full(linv[0], y_out[:half])
        low = dot_full(linv[1], y_out[half:] - dot_full_t(reach[:, :half], top))
        low = dot_full_t(linv[1], low)
        xs[half:, :] = low
        xs[:half, :] = dot_full_t(linv[0], top - dot_full(reach[:, :half], low))
        for group in range(groups):
            if group != root:
                x_copy(group).start()
        out[...] = xs[root * share : (root + 1) * share, :]
        for group in range(groups):
            if group != root:
                x_copy(group).wait_send()

    @pl.when(me != root)
    def _():
        @pl.when(me > 0)
        def _():
            for copy in up_s_copies:
                copy.wait_send()
            up_y_copy.wait_send()

    @pl.when(jnp.logical_not(odd))
    def _():
        for copy in leaf_s_copies:
            copy.wait_send()
        leaf_y_copy.wait_send()

    @pl.when(me != root)
    def _():
        x_copy(0 if root else 1).wait_recv()
        out[...] = rows_in[...]


def body(leaf_blocks, leaf_rhs, bases, couplings):
    groups = lax.axis_size("grp")
    rank = leaf_blocks.shape[1]
    width = leaf_rhs.shape[2]
    outside = pl.BlockSpec(memory_space=pltpu.HBM)
    return pl.pallas_call(
        functools.partial(kernel, groups, rank),
        out_shape=jax.ShapeDtypeStruct((rank // groups, width), F32),
        in_specs=[outside] * 4,
        out_specs=pl.BlockSpec(memory_space=pltpu.VMEM),
        scratch_shapes=[
            pltpu.VMEM((2, rank, rank), F32),
            pltpu.VMEM((2, rank, width), F32),
            pltpu.VMEM((2 * rank, 2 * rank), BF16),
            pltpu.VMEM((2 * rank, 2 * rank), BF16),
            pltpu.VMEM((rank, rank), BF16),
            pltpu.VMEM((2 * rank, 2 * rank), F32),
            pltpu.VMEM((2 * rank, 2 * rank), F32),
            pltpu.VMEM((2 * rank, 2 * rank), F32),
            pltpu.VMEM((rank // 2, rank // 2), F32),
            pltpu.VMEM((2, rank // 2, rank // 2), F32),
            pltpu.VMEM((rank // 2, 3 * rank // 2), F32),
            pltpu.VMEM((rank, rank), F32),
            pltpu.VMEM((rank, rank), F32),
            pltpu.VMEM((rank, width), F32),
            pltpu.VMEM((rank, width), F32),
            pltpu.VMEM((rank // groups, width), F32),
            pltpu.SemaphoreType.DMA((4,)),
            pltpu.SemaphoreType.DMA((2,)),
            pltpu.SemaphoreType.DMA((2, 2)),
            pltpu.SemaphoreType.DMA,
            pltpu.SemaphoreType.DMA((2,)),
            pltpu.SemaphoreType.DMA((3,)),
            pltpu.SemaphoreType.DMA((groups,)),
            pltpu.SemaphoreType.DMA,
        ],
        compiler_params=pltpu.CompilerParams(
            collective_id=0, has_side_effects=True, vmem_limit_bytes=63 << 20
        ),
    )(leaf_blocks, leaf_rhs, bases, couplings)


def solution(mesh):
    placed = (
        P("grp", None, None),
        P("grp", None, "blk"),
        P("grp", None, None),
        P("grp", None, None),
    )
    return jax.shard_map(
        body, mesh=mesh, in_specs=placed, out_specs=P("grp", "blk"), check_vma=False
    )
```

```python
import functools
import jax
import jax.numpy as jnp
from jax import lax
from jax.experimental import pallas as pl
from jax.experimental.pallas import tpu as pltpu
from jax.sharding import PartitionSpec as P

F32 = jnp.float32
BF16 = jnp.bfloat16
HIGH = lax.Precision.HIGHEST
LANES = 128


def reciprocal(x):
    return pl.reciprocal(x, approx=True)


def dot(a, b):
    return jnp.dot(a, b, preferred_element_type=F32)


def dot_full(a, b):
    return jnp.dot(a, b, preferred_element_type=F32, precision=HIGH)


def dot_full_t(a, b):
    return lax.dot_general(a, b, (((0,), (0,)), ((), ())), preferred_element_type=F32, precision=HIGH)


def dot_near(a, b, contract=1):
    a_hi, a_low = pieces(a, 2)
    b_hi, b_low = pieces(b, 2)
    dims = (((contract,), (0,)), ((), ()))
    product = functools.partial(lax.dot_general, dimension_numbers=dims, preferred_element_type=F32)
    return product(a_low, b_hi) + product(a_hi, b_low) + product(a_hi, b_hi)


def pieces(x, count):
    out = []
    for _ in range(count - 1):
        part = x.astype(BF16)
        out.append(part)
        x = x - part.astype(F32)
    out.append(x.astype(BF16))
    return out


def eliminate(rows, size, at):
    rows = rows.reshape(size // 8, 8, LANES)
    sub = lax.broadcasted_iota(jnp.int32, (8, LANES), 0)
    outs = []

    def spread(x, c):
        return jnp.broadcast_to(x[c : c + 1, :], (8, LANES))

    for start in range(0, size, 8):
        m = (size - start) // 8
        cols = [jnp.broadcast_to(rows[:, :, at + start + c : at + start + c + 1], (m, 8, LANES)) for c in range(8)]
        pivots = jnp.ones((8, LANES), F32)
        for c in range(0, 8, 2):
            a, b, d = spread(cols[c][0], c), spread(cols[c + 1][0], c), spread(cols[c + 1][0], c + 1)
            det = a * d - b * b
            over_det, over_a = reciprocal(det), reciprocal(a)
            pivots = jnp.where(sub == c, a, jnp.where(sub == c + 1, det * over_a, pivots))

            def below(x):
                head = jnp.where(sub > c + 1, x[0], 0.0)[None]
                return jnp.concatenate([head, x[1:]], 0) if m > 1 else head

            left, right = below(cols[c]), below(cols[c + 1])

            def reduced(x, u, v):
                f, g = (d * u - b * v) * over_det, (a * v - b * u) * over_det
                return x - (left * f[None] + right * g[None])

            for e in range(c + 2, 8):
                cols[e] = reduced(cols[e], spread(cols[e][0], c), spread(cols[e][0], c + 1))
            u = spread(rows[0], c)
            rows = reduced(rows, u, spread(rows[0], c + 1))
            head = jnp.where(sub == c + 1, rows[0] - (b * over_a) * u, rows[0])[None]
            rows = jnp.concatenate([head, rows[1:]], 0) if m > 1 else head
        outs.append(rows[0] * lax.rsqrt(pivots))
        rows = rows[1:]
    return jnp.concatenate(outs, 0)


def kernel(
    groups, rank, leaf_s, leaf_y, base, link, out,
    s_in, y_in, w, w_t, b, mix, cross, upper, panel, blocks, lead, trail, joint, linv, reach, vee, s_out, y_out, xs, rows_in,
    local_sem, s_send, s_recv, y_send, y_recv, leaf_send, x_send, x_recv,
):
    me = lax.axis_index("grp")
    half = rank // 2
    root = groups // 2
    share = rank // groups
    odd = lax.rem(me, 2) == 1
    step = jnp.int32(1)
    bits = groups.bit_length() - 1
    for bit in range(bits):
        step = jnp.where(lax.rem(me, 2 << bit) == 1 << bit, 1 << bit, step)
    second = lax.rem(me // (2 * step), 2)
    target = me + step - 2 * step * second

    def remote(src, dst, send, recv, group):
        return pltpu.make_async_remote_copy(
            src_ref=src, dst_ref=dst, send_sem=send, recv_sem=recv,
            device_id={"grp": group}, device_id_type=pl.DeviceIdType.MESH,
        )

    cuts = ((pl.ds(0, half), pl.ds(0, rank)), (pl.ds(half, half), pl.ds(half, half)))

    def s_copies(src, sems, slot, group):
        return [
            remote(src.at[cut], s_in.at[(slot, *cut)], sems.at[k], s_recv.at[slot, k], group)
            for k, cut in enumerate(cuts)
        ]

    leaf_s_copies = s_copies(leaf_s.at[0], leaf_send, 0, me + 1)
    leaf_y_copy = remote(leaf_y.at[0], y_in.at[0], leaf_send.at[2], y_recv.at[0], me + 1)
    up_s_copies = s_copies(s_out, s_send, second, target)
    up_y_copy = remote(y_out, y_in.at[second], y_send, y_recv.at[second], target)
    own_s = pltpu.make_async_copy(leaf_s.at[0], s_in.at[1], local_sem.at[0])
    own_y = pltpu.make_async_copy(leaf_y.at[0], y_in.at[1], local_sem.at[1])
    own_w = pltpu.make_async_copy(base.at[0], w, local_sem.at[2])
    own_b = pltpu.make_async_copy(link.at[0], b, local_sem.at[3])

    barrier = pltpu.get_barrier_semaphore()

    def greet(group):
        pl.semaphore_signal(barrier, inc=1, device_id={"grp": group}, device_id_type=pl.DeviceIdType.MESH)

    @pl.when(odd)
    def _():
        greet(me - 1)
        own_s.start()

    for bit in range(1, bits):
        @pl.when(lax.rem(me, 2 << bit) == 1 << bit)
        def _():
            lean = 0 if bit == 1 else 1
            greet(me - (1 << bit) // 2 + lean)
            greet(me + (1 << bit) // 2 + lean)

    @pl.when(jnp.logical_not(odd))
    def _():
        pl.semaphore_wait(barrier, 1)
        for copy in leaf_s_copies:
            copy.start()
        leaf_y_copy.start()

    own_w.start()
    own_b.start()

    @pl.when(odd)
    def _():
        own_y.start()

    own_w.wait()
    own_b.wait()

    small = half // 2
    same = lax.broadcasted_iota(jnp.int32, (small, half), 0) == lax.rem(lax.broadcasted_iota(jnp.int32, (small, half), 1), small)
    lane = lax.broadcasted_iota(jnp.int32, (small, half), 1)
    eye = jnp.where(same, 1.0, 0.0).astype(F32)

    def factor():
        panel[:, :half] = upper[:half, :half]
        panel[:, half:] = upper[:half, half:]

        def turn(part, carry):
            first = eliminate(jnp.where(lane < small, panel[:small, :half], eye), small, 0)[:, small:]
            lead[part] = first
            top = dot_full(first, panel[:small, :])
            joint[part] = top[:, :half]
            rest = panel[small:, :] - dot_full_t(top[:, small:half], top)
            second = eliminate(jnp.where(lane < small, eye, rest[:, :half]), small, small)[:, :small]
            trail[part] = second
            low = dot_full(second, rest[:, half:])
            blocks[:small, :] = top[:, half:]
            blocks[small:, :] = low
            vee[pl.ds(pl.multiple_of(part * half, half), half), :] = blocks[:, half:]

            @pl.when(part == 0)
            def _():
                reach[...] = blocks[:, :half]
                panel[:, :half] = upper[half:rank, half:rank] - dot_full_t(reach[...], reach[...])
                panel[:, rank:] = upper[half:rank, rank:] - dot_full_t(reach[...], vee[:half, :])

            return carry

        lax.fori_loop(0, 2, turn, 0)

    def inverses(parts):
        for part in parts:
            corner = dot_near(trail[part], dot_near(joint[part], lead[part], 0)[small:])
            linv[part, :small, :] = jnp.concatenate([lead[part], jnp.zeros((small, small), F32)], 1)
            linv[part, small:, :] = jnp.concatenate([-corner, trail[part]], 1)

    @pl.when(me > 0)
    def _():
        w_t[...] = w[...].T
        cross[:rank, :] = dot(b[...], w[rank:, :])
        cross[rank:, :] = lax.dot_general(b[...], w[:rank, :], (((0,), (0,)), ((), ())), preferred_element_type=F32)
        for copy in s_copies(s_out, s_send, 0, target):
            copy.wait_recv()

        @pl.when(odd)
        def _():
            own_s.wait()

        @pl.when(jnp.logical_not(odd))
        def _():
            for copy in s_copies(s_out, s_send, 1, target):
                copy.wait_recv()

        for slot in (0, 1):
            at = slot * rank
            s_in[slot, half:, :half] = s_in[slot, :half, half:].T
            hi, mid, low = pieces(s_in[slot], 3)
            own = w[at : at + rank, :]
            mix[at : at + rank, :] = dot(low, own) + dot(mid, own) + cross[at : at + rank, :] + dot(hi, own)
        hi, mid, low = pieces(mix[...], 3)
        upper[:rank, :] = dot(w_t[:rank, :], low) + dot(w_t[:rank, :], mid) + dot(w_t[:rank, :], hi)
        lower = w_t[rank:, :]
        upper[rank:, rank:] = dot(lower, low[:, rank:]) + dot(lower, mid[:, rank:]) + dot(lower, hi[:, rank:])
        factor()

        @pl.when(odd)
        def _():
            extra = lax.rem(me, 4) == 3
            for bit in range(3, bits):
                for sign in (-1, 1):
                    for owner in range(1 << bit, groups, 2 << bit):
                        extra = extra | (me == owner + sign * (1 << bit) // 2 + 1)
            pl.semaphore_wait(barrier, jnp.where(extra, 2, 1))

        s_out[:half, :] = upper[rank : rank + half, rank:] - dot_full_t(vee[:, :half], vee[...])

        @pl.when(me != root)
        def _():
            up_s_copies[0].start()

        s_out[half:, half:] = upper[rank + half :, rank + half :] - dot_full_t(vee[:, half:], vee[:, half:])

        @pl.when(me != root)
        def _():
            up_s_copies[1].start()

        remote(y_out, y_in.at[0], y_send, y_recv.at[0], target).wait_recv()

        @pl.when(odd)
        def _():
            own_y.wait()

        @pl.when(jnp.logical_not(odd))
        def _():
            remote(y_out, y_in.at[1], y_send, y_recv.at[1], target).wait_recv()

        inverses((0, 1))
        mixed = jnp.zeros((2 * rank, y_in.shape[2]), F32)
        for slot in (0, 1):
            hi, low = pieces(y_in[slot], 2)
            cut = w_t[:, slot * rank : (slot + 1) * rank]
            mixed = mixed + (dot(cut, low) + dot(cut, hi))
        top = dot_near(linv[0], mixed[:half])
        low = dot_near(linv[1], mixed[half:rank] - dot_near(reach[...], top, 0))
        y_out[...] = mixed[rank:] - dot_near(vee[...], jnp.concatenate([top, low], 0), 0)

        @pl.when(me != root)
        def _():
            up_y_copy.start()

    def x_copy(group):
        return remote(xs.at[pl.ds(group * share, share), :], rows_in, x_send.at[group], x_recv, group)

    @pl.when(me == root)
    def _():
        s_out[half:, :half] = s_out[:half, half:].T
        upper[:rank, :rank] = s_out[...]
        upper[:rank, rank:] = y_out[...]
        factor()
        inverses((1, 0))
        low = dot_near(linv[1], vee[half:, :], 0)
        xs[half:, :] = low
        xs[:half, :] = dot_near(linv[0], vee[:half, :] - dot_near(reach[...], low), 0)
        for group in range(groups):
            if group != root:
                x_copy(group).start()
        out[...] = xs[root * share : (root + 1) * share, :]
        for group in range(groups):
            if group != root:
                x_copy(group).wait_send()

    @pl.when(me != root)
    def _():
        @pl.when(me > 0)
        def _():
            for copy in up_s_copies:
                copy.wait_send()
            up_y_copy.wait_send()

    @pl.when(jnp.logical_not(odd))
    def _():
        for copy in leaf_s_copies:
            copy.wait_send()
        leaf_y_copy.wait_send()

    @pl.when(me != root)
    def _():
        x_copy(0 if root else 1).wait_recv()
        out[...] = rows_in[...]


def body(leaf_blocks, leaf_rhs, bases, couplings):
    groups = lax.axis_size("grp")
    rank = leaf_blocks.shape[1]
    width = leaf_rhs.shape[2]
    outside = pl.BlockSpec(memory_space=pltpu.HBM)
    return pl.pallas_call(
        functools.partial(kernel, groups, rank),
        out_shape=jax.ShapeDtypeStruct((rank // groups, width), F32),
        in_specs=[outside] * 4,
        out_specs=pl.BlockSpec(memory_space=pltpu.VMEM),
        scratch_shapes=[
            pltpu.VMEM((2, rank, rank), F32),
            pltpu.VMEM((2, rank, width), F32),
            pltpu.VMEM((2 * rank, 2 * rank), BF16),
            pltpu.VMEM((2 * rank, 2 * rank), BF16),
            pltpu.VMEM((rank, rank), BF16),
            pltpu.VMEM((2 * rank, 2 * rank), F32),
            pltpu.VMEM((2 * rank, 2 * rank), F32),
            pltpu.VMEM((2 * rank, 2 * rank), F32),
            pltpu.VMEM((rank // 2, 2 * rank), F32),
            pltpu.VMEM((rank // 2, 3 * rank // 2), F32),
            pltpu.VMEM((2, rank // 4, rank // 4), F32),
            pltpu.VMEM((2, rank // 4, rank // 4), F32),
            pltpu.VMEM((2, rank // 4, rank // 2), F32),
            pltpu.VMEM((2, rank // 2, rank // 2), F32),
            pltpu.VMEM((rank // 2, rank // 2), F32),
            pltpu.VMEM((rank, rank), F32),
            pltpu.VMEM((rank, rank), F32),
            pltpu.VMEM((rank, width), F32),
            pltpu.VMEM((rank, width), F32),
            pltpu.VMEM((rank // groups, width), F32),
            pltpu.SemaphoreType.DMA((4,)),
            pltpu.SemaphoreType.DMA((2,)),
            pltpu.SemaphoreType.DMA((2, 2)),
            pltpu.SemaphoreType.DMA,
            pltpu.SemaphoreType.DMA((2,)),
            pltpu.SemaphoreType.DMA((3,)),
            pltpu.SemaphoreType.DMA((groups,)),
            pltpu.SemaphoreType.DMA,
        ],
        compiler_params=pltpu.CompilerParams(
            collective_id=0, has_side_effects=True, vmem_limit_bytes=63 << 20
        ),
    )(leaf_blocks, leaf_rhs, bases, couplings)


def solution(mesh):
    placed = (
        P("grp", None, None),
        P("grp", None, "blk"),
        P("grp", None, None),
        P("grp", None, None),
    )
    return jax.shard_map(
        body, mesh=mesh, in_specs=placed, out_specs=P("grp", "blk"), check_vma=False
    )
```

```python
import functools
import jax
import jax.numpy as jnp
from jax import lax
from jax.experimental import pallas as pl
from jax.experimental.pallas import tpu as pltpu
from jax.sharding import PartitionSpec as P

F32 = jnp.float32
BF16 = jnp.bfloat16
HIGH = lax.Precision.HIGHEST
LANES = 128


def reciprocal(x):
    return pl.reciprocal(x, approx=True)


def dot(a, b):
    return jnp.dot(a, b, preferred_element_type=F32)


def dot_full(a, b):
    return jnp.dot(a, b, preferred_element_type=F32, precision=HIGH)


def dot_full_t(a, b):
    return lax.dot_general(a, b, (((0,), (0,)), ((), ())), preferred_element_type=F32, precision=HIGH)


def dot_near(a, b, contract=1):
    a_hi, a_low = pieces(a, 2)
    b_hi, b_low = pieces(b, 2)
    dims = (((contract,), (0,)), ((), ()))
    product = functools.partial(lax.dot_general, dimension_numbers=dims, preferred_element_type=F32)
    return product(a_low, b_hi) + product(a_hi, b_low) + product(a_hi, b_hi)


def pieces(x, count):
    out = []
    for _ in range(count - 1):
        part = x.astype(BF16)
        out.append(part)
        x = x - part.astype(F32)
    out.append(x.astype(BF16))
    return out


def eliminate(rows, size, at):
    rows = rows.reshape(size // 8, 8, LANES)
    sub = lax.broadcasted_iota(jnp.int32, (8, LANES), 0)
    outs = []

    def spread(x, c):
        return jnp.broadcast_to(x[c : c + 1, :], (8, LANES))

    def lanes(x, first):
        return [jnp.broadcast_to(x[:, :, first + c : first + c + 1], x.shape) for c in range(8)]

    head = lanes(rows[:1], at)
    for start in range(0, size, 8):
        m = (size - start) // 8
        cols = head
        if m > 1:
            cols = [jnp.concatenate([h, t], 0) for h, t in zip(head, lanes(rows[1:], at + start))]
            head = lanes(rows[1:2], at + start + 8)
        pivots = jnp.ones((8, LANES), F32)
        for c in range(0, 8, 2):
            a, b, d = spread(cols[c][0], c), spread(cols[c + 1][0], c), spread(cols[c + 1][0], c + 1)
            det = a * d - b * b
            over_det, over_a = reciprocal(det), reciprocal(a)
            pivots = jnp.where(sub == c, a, jnp.where(sub == c + 1, det * over_a, pivots))

            def below(x):
                h = jnp.where(sub > c + 1, x[0], 0.0)[None]
                return jnp.concatenate([h, x[1:]], 0) if m > 1 else h

            left, right = below(cols[c]), below(cols[c + 1])

            def factors(u, v):
                return (d * u - b * v) * over_det, (a * v - b * u) * over_det

            f, g = factors(left[0], right[0])
            for e in range(c + 2, 8):
                cols[e] = cols[e] - (left * spread(f, e)[None] + right * spread(g, e)[None])
            if m > 1:
                f, g = factors(left[1], right[1])
                for e in range(8):
                    head[e] = head[e] - (left[1:2] * spread(f, e)[None] + right[1:2] * spread(g, e)[None])
            u = spread(rows[0], c)
            f, g = factors(u, spread(rows[0], c + 1))
            rows = rows - (left * f[None] + right * g[None])
            h = jnp.where(sub == c + 1, rows[0] - (b * over_a) * u, rows[0])[None]
            rows = jnp.concatenate([h, rows[1:]], 0) if m > 1 else h
        outs.append(rows[0] * lax.rsqrt(pivots))
        rows = rows[1:]
    return jnp.concatenate(outs, 0)


def kernel(
    groups, rank, leaf_s, leaf_y, base, link, out,
    s_in, y_in, w, w_t, b, mix, cross, upper, lead, trail, joint, linv, reach, vee, s_out, y_out, xs, rows_in,
    local_sem, s_send, s_recv, y_send, y_recv, leaf_send, x_send, x_recv,
):
    me = lax.axis_index("grp")
    half = rank // 2
    root = groups // 2
    share = rank // groups
    odd = lax.rem(me, 2) == 1
    step = jnp.int32(1)
    bits = groups.bit_length() - 1
    for bit in range(bits):
        step = jnp.where(lax.rem(me, 2 << bit) == 1 << bit, 1 << bit, step)
    second = lax.rem(me // (2 * step), 2)
    target = me + step - 2 * step * second

    def remote(src, dst, send, recv, group):
        return pltpu.make_async_remote_copy(
            src_ref=src, dst_ref=dst, send_sem=send, recv_sem=recv,
            device_id={"grp": group}, device_id_type=pl.DeviceIdType.MESH,
        )

    cuts = ((pl.ds(0, half), pl.ds(0, rank)), (pl.ds(half, half), pl.ds(half, half)))

    def s_copies(src, sems, slot, group):
        return [
            remote(src.at[cut], s_in.at[(slot, *cut)], sems.at[k], s_recv.at[slot, k], group)
            for k, cut in enumerate(cuts)
        ]

    leaf_s_copies = s_copies(leaf_s.at[0], leaf_send, 0, me + 1)
    leaf_y_copy = remote(leaf_y.at[0], y_in.at[0], leaf_send.at[2], y_recv.at[0], me + 1)
    up_s_copies = s_copies(s_out, s_send, second, target)
    up_y_copy = remote(y_out, y_in.at[second], y_send, y_recv.at[second], target)
    own_s = pltpu.make_async_copy(leaf_s.at[0], s_in.at[1], local_sem.at[0])
    own_y = pltpu.make_async_copy(leaf_y.at[0], y_in.at[1], local_sem.at[1])
    own_w = pltpu.make_async_copy(base.at[0], w, local_sem.at[2])
    own_b = pltpu.make_async_copy(link.at[0], b, local_sem.at[3])

    barrier = pltpu.get_barrier_semaphore()

    def greet(group):
        pl.semaphore_signal(barrier, inc=1, device_id={"grp": group}, device_id_type=pl.DeviceIdType.MESH)

    @pl.when(odd)
    def _():
        greet(me - 1)
        own_s.start()

    for bit in range(1, bits):
        @pl.when(lax.rem(me, 2 << bit) == 1 << bit)
        def _():
            lean = 0 if bit == 1 else 1
            greet(me - (1 << bit) // 2 + lean)
            greet(me + (1 << bit) // 2 + lean)

    @pl.when(jnp.logical_not(odd))
    def _():
        pl.semaphore_wait(barrier, 1)
        for copy in leaf_s_copies:
            copy.start()
        leaf_y_copy.start()

    own_w.start()
    own_b.start()

    @pl.when(odd)
    def _():
        own_y.start()

    own_w.wait()
    own_b.wait()

    small = half // 2
    same = lax.broadcasted_iota(jnp.int32, (small, half), 0) == lax.rem(lax.broadcasted_iota(jnp.int32, (small, half), 1), small)
    lane = lax.broadcasted_iota(jnp.int32, (small, half), 1)
    eye = jnp.where(same, 1.0, 0.0).astype(F32)

    def factor():
        diag = upper[:half, :half]
        for part in (0, 1):
            first = eliminate(jnp.where(lane < small, diag[:small], eye), small, 0)[:, small:]
            lead[part] = first
            top = dot_full(first, diag[:small])
            joint[part] = top
            rest = diag[small:] - dot_full_t(top[:, small:], top)
            second = eliminate(jnp.where(lane < small, eye, rest), small, small)[:, :small]
            trail[part] = second
            if part == 0:
                side = upper[:half, half:rank]
                across = dot_full(first, side[:small])
                low = dot_full(second, side[small:] - dot_full_t(top[:, small:], across))
                reach[:small, :] = across
                reach[small:, :] = low
                diag = upper[half:rank, half:rank] - dot_full_t(reach[...], reach[...])
                side = upper[:half, rank:]
            else:
                side = upper[half:rank, rank:] - dot_full_t(reach[...], vee[:half, :])
            across = dot_full(first, side[:small])
            low = dot_full(second, side[small:] - dot_full_t(top[:, small:], across))
            vee[part * half : part * half + small, :] = across
            vee[part * half + small : (part + 1) * half, :] = low

    def inverses(parts):
        for part in parts:
            corner = dot_near(trail[part], dot_near(joint[part], lead[part], 0)[small:])
            linv[part, :small, :] = jnp.concatenate([lead[part], jnp.zeros((small, small), F32)], 1)
            linv[part, small:, :] = jnp.concatenate([-corner, trail[part]], 1)

    def side_work():
        inverses((0, 1))
        mixed = jnp.zeros((2 * rank, y_in.shape[2]), F32)
        for slot in (0, 1):
            hi, low = pieces(y_in[slot], 2)
            cut = w_t[:, slot * rank : (slot + 1) * rank]
            mixed = mixed + (dot(cut, low) + dot(cut, hi))
        top = dot_near(linv[0], mixed[:half])
        low = dot_near(linv[1], mixed[half:rank] - dot_near(reach[...], top, 0))
        y_out[...] = mixed[rank:] - dot_near(vee[...], jnp.concatenate([top, low], 0), 0)

    @pl.when(me > 0)
    def _():
        w_t[...] = w[...].T
        cross[:rank, :] = dot(b[...], w[rank:, :])
        cross[rank:, :] = lax.dot_general(b[...], w[:rank, :], (((0,), (0,)), ((), ())), preferred_element_type=F32)
        for slot in (1, 0):
            at = slot * rank
            arrivals = s_copies(s_out, s_send, slot, target)
            for k in (0, 1):
                if slot == 0:
                    arrivals[k].wait_recv()
                else:
                    @pl.when(jnp.logical_not(odd))
                    def _():
                        arrivals[k].wait_recv()

                    if k == 0:
                        @pl.when(odd)
                        def _():
                            own_s.wait()

                if k == 1:
                    s_in[slot, half:, :half] = s_in[slot, :half, half:].T
                now = slice(at + k * half, at + (k + 1) * half)
                hi, mid, low = pieces(s_in[slot, k * half : (k + 1) * half, :], 3)
                own = w[at : at + rank, :]
                mix[now, :] = dot(low, own) + dot(mid, own) + cross[now, :] + dot(hi, own)
        hi, mid, low = pieces(mix[:, :rank], 3)
        upper[:rank, :rank] = dot(w_t[:rank, :], low) + dot(w_t[:rank, :], mid) + dot(w_t[:rank, :], hi)
        hi, mid, low = pieces(mix[:, rank:], 3)
        upper[:rank, rank:] = dot(w_t[:rank, :], low) + dot(w_t[:rank, :], mid) + dot(w_t[:rank, :], hi)
        upper[rank:, rank:] = dot(w_t[rank:, :], low) + dot(w_t[rank:, :], mid) + dot(w_t[rank:, :], hi)
        factor()

        @pl.when(odd)
        def _():
            extra = lax.rem(me, 4) == 3
            for bit in range(3, bits):
                for sign in (-1, 1):
                    for owner in range(1 << bit, groups, 2 << bit):
                        extra = extra | (me == owner + sign * (1 << bit) // 2 + 1)
            pl.semaphore_wait(barrier, jnp.where(extra, 2, 1))

        s_out[:half, :] = upper[rank : rank + half, rank:] - dot_full_t(vee[:, :half], vee[...])

        @pl.when(me != root)
        def _():
            up_s_copies[0].start()

        s_out[half:, half:] = upper[rank + half :, rank + half :] - dot_full_t(vee[:, half:], vee[:, half:])

        @pl.when(me != root)
        def _():
            up_s_copies[1].start()

        remote(y_out, y_in.at[0], y_send, y_recv.at[0], target).wait_recv()

        @pl.when(odd)
        def _():
            own_y.wait()

        @pl.when(jnp.logical_not(odd))
        def _():
            remote(y_out, y_in.at[1], y_send, y_recv.at[1], target).wait_recv()

        @pl.when(me != root)
        def _():
            side_work()
            up_y_copy.start()

    def x_copy(group):
        return remote(xs.at[pl.ds(group * share, share), :], rows_in, x_send.at[group], x_recv, group)

    @pl.when(me == root)
    def _():
        side_work()
        s_out[half:, :half] = s_out[:half, half:].T
        upper[:rank, :rank] = s_out[...]
        upper[:rank, rank:] = y_out[...]
        factor()
        inverses((1, 0))
        low = dot_near(linv[1], vee[half:, :], 0)
        xs[half:, :] = low
        xs[:half, :] = dot_near(linv[0], vee[:half, :] - dot_near(reach[...], low), 0)
        for group in range(groups):
            if group != root:
                x_copy(group).start()
        out[...] = xs[root * share : (root + 1) * share, :]
        for group in range(groups):
            if group != root:
                x_copy(group).wait_send()

    @pl.when(me != root)
    def _():
        @pl.when(me > 0)
        def _():
            for copy in up_s_copies:
                copy.wait_send()
            up_y_copy.wait_send()

    @pl.when(jnp.logical_not(odd))
    def _():
        for copy in leaf_s_copies:
            copy.wait_send()
        leaf_y_copy.wait_send()

    @pl.when(me != root)
    def _():
        x_copy(0 if root else 1).wait_recv()
        out[...] = rows_in[...]


def body(leaf_blocks, leaf_rhs, bases, couplings):
    groups = lax.axis_size("grp")
    rank = leaf_blocks.shape[1]
    width = leaf_rhs.shape[2]
    outside = pl.BlockSpec(memory_space=pltpu.HBM)
    return pl.pallas_call(
        functools.partial(kernel, groups, rank),
        out_shape=jax.ShapeDtypeStruct((rank // groups, width), F32),
        in_specs=[outside] * 4,
        out_specs=pl.BlockSpec(memory_space=pltpu.VMEM),
        scratch_shapes=[
            pltpu.VMEM((2, rank, rank), F32),
            pltpu.VMEM((2, rank, width), F32),
            pltpu.VMEM((2 * rank, 2 * rank), BF16),
            pltpu.VMEM((2 * rank, 2 * rank), BF16),
            pltpu.VMEM((rank, rank), BF16),
            pltpu.VMEM((2 * rank, 2 * rank), F32),
            pltpu.VMEM((2 * rank, 2 * rank), F32),
            pltpu.VMEM((2 * rank, 2 * rank), F32),
            pltpu.VMEM((2, rank // 4, rank // 4), F32),
            pltpu.VMEM((2, rank // 4, rank // 4), F32),
            pltpu.VMEM((2, rank // 4, rank // 2), F32),
            pltpu.VMEM((2, rank // 2, rank // 2), F32),
            pltpu.VMEM((rank // 2, rank // 2), F32),
            pltpu.VMEM((rank, rank), F32),
            pltpu.VMEM((rank, rank), F32),
            pltpu.VMEM((rank, width), F32),
            pltpu.VMEM((rank, width), F32),
            pltpu.VMEM((rank // groups, width), F32),
            pltpu.SemaphoreType.DMA((4,)),
            pltpu.SemaphoreType.DMA((2,)),
            pltpu.SemaphoreType.DMA((2, 2)),
            pltpu.SemaphoreType.DMA,
            pltpu.SemaphoreType.DMA((2,)),
            pltpu.SemaphoreType.DMA((3,)),
            pltpu.SemaphoreType.DMA((groups,)),
            pltpu.SemaphoreType.DMA,
        ],
        compiler_params=pltpu.CompilerParams(
            collective_id=0, has_side_effects=True, vmem_limit_bytes=63 << 20
        ),
    )(leaf_blocks, leaf_rhs, bases, couplings)


def solution(mesh):
    placed = (
        P("grp", None, None),
        P("grp", None, "blk"),
        P("grp", None, None),
        P("grp", None, None),
    )
    return jax.shard_map(
        body, mesh=mesh, in_specs=placed, out_specs=P("grp", "blk"), check_vma=False
    )
```

```python
import functools
import jax
import jax.numpy as jnp
from jax import lax
from jax.experimental import pallas as pl
from jax.experimental.pallas import tpu as pltpu
from jax.sharding import PartitionSpec as P

F32 = jnp.float32
BF16 = jnp.bfloat16
HIGH = lax.Precision.HIGHEST
LANES = 128


def reciprocal(x):
    return pl.reciprocal(x, approx=True)


def dot(a, b):
    return jnp.dot(a, b, preferred_element_type=F32)


def dot_full(a, b):
    return jnp.dot(a, b, preferred_element_type=F32, precision=HIGH)


def dot_full_t(a, b):
    return lax.dot_general(a, b, (((0,), (0,)), ((), ())), preferred_element_type=F32, precision=HIGH)


def dot_near(a, b, contract=1):
    a_hi, a_low = pieces(a, 2)
    b_hi, b_low = pieces(b, 2)
    dims = (((contract,), (0,)), ((), ()))
    product = functools.partial(lax.dot_general, dimension_numbers=dims, preferred_element_type=F32)
    return product(a_low, b_hi) + product(a_hi, b_low) + product(a_hi, b_hi)


def pieces(x, count):
    out = []
    for _ in range(count - 1):
        part = x.astype(BF16)
        out.append(part)
        x = x - part.astype(F32)
    out.append(x.astype(BF16))
    return out


def eliminate(rows, size, at):
    rows = rows.reshape(size // 8, 8, LANES)
    sub = lax.broadcasted_iota(jnp.int32, (8, LANES), 0)
    outs = []

    def spread(x, c):
        return jnp.broadcast_to(x[c : c + 1, :], (8, LANES))

    def lanes(x, first):
        return [jnp.broadcast_to(x[:, :, first + c : first + c + 1], x.shape) for c in range(8)]

    head = lanes(rows[:1], at)
    for start in range(0, size, 8):
        m = (size - start) // 8
        cols = head
        if m > 1:
            cols = [jnp.concatenate([h, t], 0) for h, t in zip(head, lanes(rows[1:], at + start))]
            head = lanes(rows[1:2], at + start + 8)
        pivots = jnp.ones((8, LANES), F32)
        for c in range(0, 8, 2):
            a, b, d = spread(cols[c][0], c), spread(cols[c + 1][0], c), spread(cols[c + 1][0], c + 1)
            det = a * d - b * b
            over_det, over_a = reciprocal(det), reciprocal(a)
            pivots = jnp.where(sub == c, a, jnp.where(sub == c + 1, det * over_a, pivots))

            def below(x):
                h = jnp.where(sub > c + 1, x[0], 0.0)[None]
                return jnp.concatenate([h, x[1:]], 0) if m > 1 else h

            left, right = below(cols[c]), below(cols[c + 1])

            def factors(u, v):
                return (d * u - b * v) * over_det, (a * v - b * u) * over_det

            f, g = factors(left[0], right[0])
            for e in range(c + 2, 8):
                cols[e] = cols[e] - (left * spread(f, e)[None] + right * spread(g, e)[None])
            if m > 1:
                f, g = factors(left[1], right[1])
                for e in range(8):
                    head[e] = head[e] - (left[1:2] * spread(f, e)[None] + right[1:2] * spread(g, e)[None])
            u = spread(rows[0], c)
            f, g = factors(u, spread(rows[0], c + 1))
            rows = rows - (left * f[None] + right * g[None])
            h = jnp.where(sub == c + 1, rows[0] - (b * over_a) * u, rows[0])[None]
            rows = jnp.concatenate([h, rows[1:]], 0) if m > 1 else h
        outs.append(rows[0] * lax.rsqrt(pivots))
        rows = rows[1:]
    return jnp.concatenate(outs, 0)


def kernel(
    groups, rank, leaf_s, leaf_y, base, link, out,
    s_in, y_in, w, w_t, b, mix, cross, upper, lead, trail, joint, linv, reach, vee, s_out, y_out, xs, rows_in,
    local_sem, s_send, s_recv, y_send, y_recv, leaf_send, x_send, x_recv,
):
    me = lax.axis_index("grp")
    half = rank // 2
    root = groups // 2
    share = rank // groups
    odd = lax.rem(me, 2) == 1
    step = jnp.int32(1)
    bits = groups.bit_length() - 1
    for bit in range(bits):
        step = jnp.where(lax.rem(me, 2 << bit) == 1 << bit, 1 << bit, step)
    second = lax.rem(me // (2 * step), 2)
    target = me + step - 2 * step * second

    def remote(src, dst, send, recv, group):
        return pltpu.make_async_remote_copy(
            src_ref=src, dst_ref=dst, send_sem=send, recv_sem=recv,
            device_id={"grp": group}, device_id_type=pl.DeviceIdType.MESH,
        )

    cuts = ((pl.ds(0, half), pl.ds(0, rank)), (pl.ds(half, half), pl.ds(half, half)))

    def s_copies(src, sems, slot, group):
        return [
            remote(src.at[cut], s_in.at[(slot, *cut)], sems.at[k], s_recv.at[slot, k], group)
            for k, cut in enumerate(cuts)
        ]

    leaf_s_copies = s_copies(leaf_s.at[0], leaf_send, 0, me + 1)
    leaf_y_copy = remote(leaf_y.at[0], y_in.at[0], leaf_send.at[2], y_recv.at[0], me + 1)
    up_s_copies = s_copies(s_out, s_send, second, target)
    up_y_copy = remote(y_out, y_in.at[second], y_send, y_recv.at[second], target)
    own_s = pltpu.make_async_copy(leaf_s.at[0], s_in.at[1], local_sem.at[0])
    own_y = pltpu.make_async_copy(leaf_y.at[0], y_in.at[1], local_sem.at[1])
    own_w = pltpu.make_async_copy(base.at[0], w, local_sem.at[2])
    own_b = pltpu.make_async_copy(link.at[0], b, local_sem.at[3])

    barrier = pltpu.get_barrier_semaphore()

    def greet(group):
        pl.semaphore_signal(barrier, inc=1, device_id={"grp": group}, device_id_type=pl.DeviceIdType.MESH)

    @pl.when(odd)
    def _():
        greet(me - 1)
        own_s.start()

    for bit in range(1, bits):
        @pl.when(lax.rem(me, 2 << bit) == 1 << bit)
        def _():
            lean = 0 if bit == 1 else 1
            greet(me - (1 << bit) // 2 + lean)
            greet(me + (1 << bit) // 2 + lean)

    @pl.when(jnp.logical_not(odd))
    def _():
        pl.semaphore_wait(barrier, 1)
        for copy in leaf_s_copies:
            copy.start()
        leaf_y_copy.start()

    own_w.start()
    own_b.start()

    @pl.when(odd)
    def _():
        own_y.start()

    own_w.wait()
    own_b.wait()

    small = half // 2
    same = lax.broadcasted_iota(jnp.int32, (small, half), 0) == lax.rem(lax.broadcasted_iota(jnp.int32, (small, half), 1), small)
    lane = lax.broadcasted_iota(jnp.int32, (small, half), 1)
    eye = jnp.where(same, 1.0, 0.0).astype(F32)

    def factor(partial):
        diag = upper[:half, :half]
        for part in (0, 1):
            first = eliminate(jnp.where(lane < small, diag[:small], eye), small, 0)[:, small:]
            lead[part] = first
            top = dot_full(first, diag[:small])
            joint[part] = top
            flipped = lax.dot_general(
                diag[small:, :small], first, (((1,), (1,)), ((), ())), preferred_element_type=F32, precision=HIGH
            )
            rest = diag[small:] - dot_full(flipped, top)
            second = eliminate(jnp.where(lane < small, eye, rest), small, small)[:, :small]
            trail[part] = second
            if part == 0:
                side = upper[:half, half:rank]
                across = dot_full(first, side[:small])
                low = dot_full(second, side[small:] - dot_full_t(top[:, small:], across))
                reach[:small, :] = across
                reach[small:, :] = low
                diag = upper[half:rank, half:rank] - dot_full_t(reach[...], reach[...])
                side = upper[:half, rank:]
            else:
                side = upper[half:rank, rank:] - dot_full_t(reach[...], vee[:half, :])
                if partial:
                    mix[:half, :rank] = upper[rank : rank + half, rank:] - dot_full_t(vee[:half, :half], vee[:half, :])
                    mix[half:rank, half:rank] = upper[rank + half :, rank + half :] - dot_full_t(vee[:half, half:], vee[:half, half:])
            across = dot_full(first, side[:small])
            low = dot_full(second, side[small:] - dot_full_t(top[:, small:], across))
            vee[part * half : part * half + small, :] = across
            vee[part * half + small : (part + 1) * half, :] = low

    def inverses(parts):
        for part in parts:
            corner = dot_near(trail[part], dot_near(joint[part], lead[part], 0)[small:])
            linv[part, :small, :] = jnp.concatenate([lead[part], jnp.zeros((small, small), F32)], 1)
            linv[part, small:, :] = jnp.concatenate([-corner, trail[part]], 1)

    def side_work():
        inverses((0, 1))
        mixed = jnp.zeros((2 * rank, y_in.shape[2]), F32)
        for slot in (0, 1):
            hi, low = pieces(y_in[slot], 2)
            cut = w_t[:, slot * rank : (slot + 1) * rank]
            mixed = mixed + (dot(cut, low) + dot(cut, hi))
        top = dot_near(linv[0], mixed[:half])
        low = dot_near(linv[1], mixed[half:rank] - dot_near(reach[...], top, 0))
        y_out[...] = mixed[rank:] - dot_near(vee[...], jnp.concatenate([top, low], 0), 0)

    @pl.when(me > 0)
    def _():
        w_t[...] = w[...].T
        cross[:rank, :] = dot(b[...], w[rank:, :])
        cross[rank:, :] = lax.dot_general(b[...], w[:rank, :], (((0,), (0,)), ((), ())), preferred_element_type=F32)
        for slot in (1, 0):
            at = slot * rank
            arrivals = s_copies(s_out, s_send, slot, target)
            for k in (0, 1):
                if slot == 0:
                    arrivals[k].wait_recv()
                else:
                    @pl.when(jnp.logical_not(odd))
                    def _():
                        arrivals[k].wait_recv()

                    if k == 0:
                        @pl.when(odd)
                        def _():
                            own_s.wait()

                if k == 1:
                    s_in[slot, half:, :half] = s_in[slot, :half, half:].T
                now = slice(at + k * half, at + (k + 1) * half)
                hi, mid, low = pieces(s_in[slot, k * half : (k + 1) * half, :], 3)
                own = w[at : at + rank, :]
                mix[now, :] = dot(low, own) + dot(mid, own) + cross[now, :] + dot(hi, own)
        hi, mid, low = pieces(mix[:, :rank], 3)
        upper[:rank, :rank] = dot(w_t[:rank, :], low) + dot(w_t[:rank, :], mid) + dot(w_t[:rank, :], hi)
        hi, mid, low = pieces(mix[:, rank:], 3)
        upper[:rank, rank:] = dot(w_t[:rank, :], low) + dot(w_t[:rank, :], mid) + dot(w_t[:rank, :], hi)
        upper[rank:, rank:] = dot(w_t[rank:, :], low) + dot(w_t[rank:, :], mid) + dot(w_t[rank:, :], hi)
        factor(True)

        @pl.when(odd)
        def _():
            extra = lax.rem(me, 4) == 3
            for bit in range(3, bits):
                for sign in (-1, 1):
                    for owner in range(1 << bit, groups, 2 << bit):
                        extra = extra | (me == owner + sign * (1 << bit) // 2 + 1)
            pl.semaphore_wait(barrier, jnp.where(extra, 2, 1))

        s_out[:half, :] = mix[:half, :rank] - dot_full_t(vee[half:, :half], vee[half:, :])

        @pl.when(me != root)
        def _():
            up_s_copies[0].start()

        s_out[half:, half:] = mix[half:rank, half:rank] - dot_full_t(vee[half:, half:], vee[half:, half:])

        @pl.when(me != root)
        def _():
            up_s_copies[1].start()

        remote(y_out, y_in.at[0], y_send, y_recv.at[0], target).wait_recv()

        @pl.when(odd)
        def _():
            own_y.wait()

        @pl.when(jnp.logical_not(odd))
        def _():
            remote(y_out, y_in.at[1], y_send, y_recv.at[1], target).wait_recv()

        @pl.when(me != root)
        def _():
            side_work()
            up_y_copy.start()

    def x_copy(group):
        return remote(xs.at[pl.ds(group * share, share), :], rows_in, x_send.at[group], x_recv, group)

    @pl.when(me == root)
    def _():
        side_work()
        s_out[half:, :half] = s_out[:half, half:].T
        upper[:rank, :rank] = s_out[...]
        upper[:rank, rank:] = y_out[...]
        factor(False)
        inverses((1, 0))
        low = dot_near(linv[1], vee[half:, :], 0)
        xs[half:, :] = low
        xs[:half, :] = dot_near(linv[0], vee[:half, :] - dot_near(reach[...], low), 0)
        for group in range(groups):
            if group != root:
                x_copy(group).start()
        out[...] = xs[root * share : (root + 1) * share, :]
        for group in range(groups):
            if group != root:
                x_copy(group).wait_send()

    @pl.when(me != root)
    def _():
        @pl.when(me > 0)
        def _():
            for copy in up_s_copies:
                copy.wait_send()
            up_y_copy.wait_send()

    @pl.when(jnp.logical_not(odd))
    def _():
        for copy in leaf_s_copies:
            copy.wait_send()
        leaf_y_copy.wait_send()

    @pl.when(me != root)
    def _():
        x_copy(0 if root else 1).wait_recv()
        out[...] = rows_in[...]


def body(leaf_blocks, leaf_rhs, bases, couplings):
    groups = lax.axis_size("grp")
    rank = leaf_blocks.shape[1]
    width = leaf_rhs.shape[2]
    outside = pl.BlockSpec(memory_space=pltpu.HBM)
    return pl.pallas_call(
        functools.partial(kernel, groups, rank),
        out_shape=jax.ShapeDtypeStruct((rank // groups, width), F32),
        in_specs=[outside] * 4,
        out_specs=pl.BlockSpec(memory_space=pltpu.VMEM),
        scratch_shapes=[
            pltpu.VMEM((2, rank, rank), F32),
            pltpu.VMEM((2, rank, width), F32),
            pltpu.VMEM((2 * rank, 2 * rank), BF16),
            pltpu.VMEM((2 * rank, 2 * rank), BF16),
            pltpu.VMEM((rank, rank), BF16),
            pltpu.VMEM((2 * rank, 2 * rank), F32),
            pltpu.VMEM((2 * rank, 2 * rank), F32),
            pltpu.VMEM((2 * rank, 2 * rank), F32),
            pltpu.VMEM((2, rank // 4, rank // 4), F32),
            pltpu.VMEM((2, rank // 4, rank // 4), F32),
            pltpu.VMEM((2, rank // 4, rank // 2), F32),
            pltpu.VMEM((2, rank // 2, rank // 2), F32),
            pltpu.VMEM((rank // 2, rank // 2), F32),
            pltpu.VMEM((rank, rank), F32),
            pltpu.VMEM((rank, rank), F32),
            pltpu.VMEM((rank, width), F32),
            pltpu.VMEM((rank, width), F32),
            pltpu.VMEM((rank // groups, width), F32),
            pltpu.SemaphoreType.DMA((4,)),
            pltpu.SemaphoreType.DMA((2,)),
            pltpu.SemaphoreType.DMA((2, 2)),
            pltpu.SemaphoreType.DMA,
            pltpu.SemaphoreType.DMA((2,)),
            pltpu.SemaphoreType.DMA((3,)),
            pltpu.SemaphoreType.DMA((groups,)),
            pltpu.SemaphoreType.DMA,
        ],
        compiler_params=pltpu.CompilerParams(
            collective_id=0, has_side_effects=True, vmem_limit_bytes=63 << 20
        ),
    )(leaf_blocks, leaf_rhs, bases, couplings)


def solution(mesh):
    placed = (
        P("grp", None, None),
        P("grp", None, "blk"),
        P("grp", None, None),
        P("grp", None, None),
    )
    return jax.shard_map(
        body, mesh=mesh, in_specs=placed, out_specs=P("grp", "blk"), check_vma=False
    )
```

```python
import functools
import jax
import jax.numpy as jnp
from jax import lax
from jax.experimental import pallas as pl
from jax.experimental.pallas import tpu as pltpu
from jax.sharding import PartitionSpec as P

F32 = jnp.float32
BF16 = jnp.bfloat16
HIGH = lax.Precision.HIGHEST
LANES = 128


def reciprocal(x):
    return pl.reciprocal(x, approx=True)


def dot(a, b):
    return jnp.dot(a, b, preferred_element_type=F32)


def dot_full(a, b):
    return jnp.dot(a, b, preferred_element_type=F32, precision=HIGH)


def dot_full_t(a, b):
    return lax.dot_general(a, b, (((0,), (0,)), ((), ())), preferred_element_type=F32, precision=HIGH)


def dot_near(a, b, contract=1):
    a_hi, a_low = pieces(a, 2)
    b_hi, b_low = pieces(b, 2)
    dims = (((contract,), (0,)), ((), ()))
    product = functools.partial(lax.dot_general, dimension_numbers=dims, preferred_element_type=F32)
    return product(a_low, b_hi) + product(a_hi, b_low) + product(a_hi, b_hi)


def pieces(x, count):
    out = []
    for _ in range(count - 1):
        part = x.astype(BF16)
        out.append(part)
        x = x - part.astype(F32)
    out.append(x.astype(BF16))
    return out


def eliminate(rows, size, at):
    rows = rows.reshape(size // 8, 8, LANES)
    sub = lax.broadcasted_iota(jnp.int32, (8, LANES), 0)
    outs = []

    def spread(x, c):
        return jnp.broadcast_to(x[c : c + 1, :], (8, LANES))

    def lanes(x, first):
        return [jnp.broadcast_to(x[:, :, first + c : first + c + 1], x.shape) for c in range(8)]

    head = lanes(rows[:1], at)
    for start in range(0, size, 8):
        m = (size - start) // 8
        cols = head
        if m > 1:
            cols = [jnp.concatenate([h, t], 0) for h, t in zip(head, lanes(rows[1:], at + start))]
            head = lanes(rows[1:2], at + start + 8)
        pivots = jnp.ones((8, LANES), F32)
        for c in range(0, 8, 2):
            a, b, d = spread(cols[c][0], c), spread(cols[c + 1][0], c), spread(cols[c + 1][0], c + 1)
            det = a * d - b * b
            over_det, over_a = reciprocal(det), reciprocal(a)
            pivots = jnp.where(sub == c, a, jnp.where(sub == c + 1, det * over_a, pivots))

            def below(x):
                h = jnp.where(sub > c + 1, x[0], 0.0)[None]
                return jnp.concatenate([h, x[1:]], 0) if m > 1 else h

            left, right = below(cols[c]), below(cols[c + 1])

            def factors(u, v):
                return (d * u - b * v) * over_det, (a * v - b * u) * over_det

            f, g = factors(left[0], right[0])
            for e in range(c + 2, 8):
                cols[e] = cols[e] - (left * spread(f, e)[None] + right * spread(g, e)[None])
            if m > 1:
                f, g = factors(left[1], right[1])
                for e in range(8):
                    head[e] = head[e] - (left[1:2] * spread(f, e)[None] + right[1:2] * spread(g, e)[None])
            u = spread(rows[0], c)
            f, g = factors(u, spread(rows[0], c + 1))
            rows = rows - (left * f[None] + right * g[None])
            h = jnp.where(sub == c + 1, rows[0] - (b * over_a) * u, rows[0])[None]
            rows = jnp.concatenate([h, rows[1:]], 0) if m > 1 else h
        outs.append(rows[0] * lax.rsqrt(pivots))
        rows = rows[1:]
    return jnp.concatenate(outs, 0)


def kernel(
    groups, rank, leaf_s, leaf_y, base, link, out,
    s_in, y_in, w, w_t, b, mix, cross, upper, lead, trail, joint, linv, reach, vee, s_out, y_out, xs, rows_in,
    local_sem, s_send, s_recv, y_send, y_recv, leaf_send, x_send, x_recv,
):
    me = lax.axis_index("grp")
    half = rank // 2
    root = groups // 2
    share = rank // groups
    odd = lax.rem(me, 2) == 1
    step = jnp.int32(1)
    bits = groups.bit_length() - 1
    for bit in range(bits):
        step = jnp.where(lax.rem(me, 2 << bit) == 1 << bit, 1 << bit, step)
    second = lax.rem(me // (2 * step), 2)
    target = me + step - 2 * step * second

    def remote(src, dst, send, recv, group):
        return pltpu.make_async_remote_copy(
            src_ref=src, dst_ref=dst, send_sem=send, recv_sem=recv,
            device_id={"grp": group}, device_id_type=pl.DeviceIdType.MESH,
        )

    quarter = half // 2
    cuts = (
        (pl.ds(0, quarter), pl.ds(0, rank)), (pl.ds(quarter, quarter), pl.ds(0, rank)), (pl.ds(half, half), pl.ds(half, half))
    )

    def s_copies(src, sems, slot, group):
        return [
            remote(src.at[cut], s_in.at[(slot, *cut)], sems.at[k], s_recv.at[slot, k], group)
            for k, cut in enumerate(cuts)
        ]

    leaf_s_copies = s_copies(leaf_s.at[0], leaf_send, 0, me + 1)
    leaf_y_copy = remote(leaf_y.at[0], y_in.at[0], leaf_send.at[3], y_recv.at[0], me + 1)
    up_s_copies = s_copies(s_out, s_send, second, target)
    up_y_copy = remote(y_out, y_in.at[second], y_send, y_recv.at[second], target)
    own_s = pltpu.make_async_copy(leaf_s.at[0], s_in.at[1], local_sem.at[0])
    own_y = pltpu.make_async_copy(leaf_y.at[0], y_in.at[1], local_sem.at[1])
    own_w = pltpu.make_async_copy(base.at[0], w, local_sem.at[2])
    own_b = pltpu.make_async_copy(link.at[0], b, local_sem.at[3])

    barrier = pltpu.get_barrier_semaphore()

    def greet(group):
        pl.semaphore_signal(barrier, inc=1, device_id={"grp": group}, device_id_type=pl.DeviceIdType.MESH)

    @pl.when(odd)
    def _():
        greet(me - 1)
        own_s.start()

    for bit in range(1, bits):
        @pl.when(lax.rem(me, 2 << bit) == 1 << bit)
        def _():
            lean = 0 if bit == 1 else 1
            greet(me - (1 << bit) // 2 + lean)
            greet(me + (1 << bit) // 2 + lean)

    @pl.when(jnp.logical_not(odd))
    def _():
        pl.semaphore_wait(barrier, 1)
        for copy in leaf_s_copies:
            copy.start()
        leaf_y_copy.start()

    own_w.start()
    own_b.start()

    @pl.when(odd)
    def _():
        own_y.start()

    own_w.wait()
    own_b.wait()

    small = half // 2
    same = lax.broadcasted_iota(jnp.int32, (small, half), 0) == lax.rem(lax.broadcasted_iota(jnp.int32, (small, half), 1), small)
    lane = lax.broadcasted_iota(jnp.int32, (small, half), 1)
    eye = jnp.where(same, 1.0, 0.0).astype(F32)

    def factor(partial):
        diag = upper[:half, :half]
        for part in (0, 1):
            first = eliminate(jnp.where(lane < small, diag[:small], eye), small, 0)[:, small:]
            lead[part] = first
            top = dot_full(first, diag[:small])
            joint[part] = top
            flipped = lax.dot_general(
                diag[small:, :small], first, (((1,), (1,)), ((), ())), preferred_element_type=F32, precision=HIGH
            )
            rest = diag[small:] - dot_full(flipped, top)
            second = eliminate(jnp.where(lane < small, eye, rest), small, small)[:, :small]
            trail[part] = second
            if part == 0:
                side = upper[:half, half:rank]
                across = dot_full(first, side[:small])
                low = dot_full(second, side[small:] - dot_full_t(top[:, small:], across))
                reach[:small, :] = across
                reach[small:, :] = low
                diag = upper[half:rank, half:rank] - dot_full_t(reach[...], reach[...])
                side = upper[:half, rank:]
            else:
                side = upper[half:rank, rank:] - dot_full_t(reach[...], vee[:half, :])
                if partial:
                    mix[:half, :rank] = upper[rank : rank + half, rank:] - dot_full_t(vee[:half, :half], vee[:half, :])
                    mix[half:rank, half:rank] = upper[rank + half :, rank + half :] - dot_full_t(vee[:half, half:], vee[:half, half:])
            across = dot_full(first, side[:small])
            low = dot_full(second, side[small:] - dot_full_t(top[:, small:], across))
            vee[part * half : part * half + small, :] = across
            vee[part * half + small : (part + 1) * half, :] = low

    def inverses(parts):
        for part in parts:
            corner = dot_near(trail[part], dot_near(joint[part], lead[part], 0)[small:])
            linv[part, :small, :] = jnp.concatenate([lead[part], jnp.zeros((small, small), F32)], 1)
            linv[part, small:, :] = jnp.concatenate([-corner, trail[part]], 1)

    def side_work():
        inverses((0, 1))
        mixed = jnp.zeros((2 * rank, y_in.shape[2]), F32)
        for slot in (0, 1):
            hi, low = pieces(y_in[slot], 2)
            cut = w_t[:, slot * rank : (slot + 1) * rank]
            mixed = mixed + (dot(cut, low) + dot(cut, hi))
        top = dot_near(linv[0], mixed[:half])
        low = dot_near(linv[1], mixed[half:rank] - dot_near(reach[...], top, 0))
        y_out[...] = mixed[rank:] - dot_near(vee[...], jnp.concatenate([top, low], 0), 0)

    @pl.when(me > 0)
    def _():
        w_t[...] = w[...].T
        cross[:rank, :] = dot(b[...], w[rank:, :])
        cross[rank:, :] = lax.dot_general(b[...], w[:rank, :], (((0,), (0,)), ((), ())), preferred_element_type=F32)
        for slot in (1, 0):
            at = slot * rank
            arrivals = s_copies(s_out, s_send, slot, target)
            for k in (0, 1):
                if slot == 0:
                    for copy in arrivals[2 * k : 2 + k]:
                        copy.wait_recv()
                else:
                    @pl.when(jnp.logical_not(odd))
                    def _():
                        for copy in arrivals[2 * k : 2 + k]:
                            copy.wait_recv()

                    if k == 0:
                        @pl.when(odd)
                        def _():
                            own_s.wait()

                if k == 1:
                    s_in[slot, half:, :half] = s_in[slot, :half, half:].T
                now = slice(at + k * half, at + (k + 1) * half)
                hi, mid, low = pieces(s_in[slot, k * half : (k + 1) * half, :], 3)
                own = w[at : at + rank, :]
                mix[now, :] = dot(low, own) + dot(mid, own) + cross[now, :] + dot(hi, own)
        hi, mid, low = pieces(mix[:, :rank], 3)
        upper[:rank, :rank] = dot(w_t[:rank, :], low) + dot(w_t[:rank, :], mid) + dot(w_t[:rank, :], hi)
        hi, mid, low = pieces(mix[:, rank:], 3)
        upper[:rank, rank:] = dot(w_t[:rank, :], low) + dot(w_t[:rank, :], mid) + dot(w_t[:rank, :], hi)
        upper[rank:, rank:] = dot(w_t[rank:, :], low) + dot(w_t[rank:, :], mid) + dot(w_t[rank:, :], hi)
        factor(True)

        @pl.when(odd)
        def _():
            extra = lax.rem(me, 4) == 3
            for bit in range(3, bits):
                for sign in (-1, 1):
                    for owner in range(1 << bit, groups, 2 << bit):
                        extra = extra | (me == owner + sign * (1 << bit) // 2 + 1)
            pl.semaphore_wait(barrier, jnp.where(extra, 2, 1))

        for k in (0, 1):
            now = slice(k * quarter, (k + 1) * quarter)
            s_out[now, :] = mix[now, :rank] - dot_full_t(vee[half:, now], vee[half:, :])

            @pl.when(me != root)
            def _():
                up_s_copies[k].start()

        s_out[half:, half:] = mix[half:rank, half:rank] - dot_full_t(vee[half:, half:], vee[half:, half:])

        @pl.when(me != root)
        def _():
            up_s_copies[2].start()

        remote(y_out, y_in.at[0], y_send, y_recv.at[0], target).wait_recv()

        @pl.when(odd)
        def _():
            own_y.wait()

        @pl.when(jnp.logical_not(odd))
        def _():
            remote(y_out, y_in.at[1], y_send, y_recv.at[1], target).wait_recv()

        @pl.when(me != root)
        def _():
            side_work()
            up_y_copy.start()

    def x_copy(group):
        return remote(xs.at[pl.ds(group * share, share), :], rows_in, x_send.at[group], x_recv, group)

    @pl.when(me == root)
    def _():
        side_work()
        s_out[half:, :half] = s_out[:half, half:].T
        upper[:rank, :rank] = s_out[...]
        upper[:rank, rank:] = y_out[...]
        factor(False)
        inverses((1, 0))
        low = dot_near(linv[1], vee[half:, :], 0)
        xs[half:, :] = low
        xs[:half, :] = dot_near(linv[0], vee[:half, :] - dot_near(reach[...], low), 0)
        for group in range(groups):
            if group != root:
                x_copy(group).start()
        out[...] = xs[root * share : (root + 1) * share, :]
        for group in range(groups):
            if group != root:
                x_copy(group).wait_send()

    @pl.when(me != root)
    def _():
        @pl.when(me > 0)
        def _():
            for copy in up_s_copies:
                copy.wait_send()
            up_y_copy.wait_send()

    @pl.when(jnp.logical_not(odd))
    def _():
        for copy in leaf_s_copies:
            copy.wait_send()
        leaf_y_copy.wait_send()

    @pl.when(me != root)
    def _():
        x_copy(0 if root else 1).wait_recv()
        out[...] = rows_in[...]


def body(leaf_blocks, leaf_rhs, bases, couplings):
    groups = lax.axis_size("grp")
    rank = leaf_blocks.shape[1]
    width = leaf_rhs.shape[2]
    outside = pl.BlockSpec(memory_space=pltpu.HBM)
    return pl.pallas_call(
        functools.partial(kernel, groups, rank),
        out_shape=jax.ShapeDtypeStruct((rank // groups, width), F32),
        in_specs=[outside] * 4,
        out_specs=pl.BlockSpec(memory_space=pltpu.VMEM),
        scratch_shapes=[
            pltpu.VMEM((2, rank, rank), F32),
            pltpu.VMEM((2, rank, width), F32),
            pltpu.VMEM((2 * rank, 2 * rank), BF16),
            pltpu.VMEM((2 * rank, 2 * rank), BF16),
            pltpu.VMEM((rank, rank), BF16),
            pltpu.VMEM((2 * rank, 2 * rank), F32),
            pltpu.VMEM((2 * rank, 2 * rank), F32),
            pltpu.VMEM((2 * rank, 2 * rank), F32),
            pltpu.VMEM((2, rank // 4, rank // 4), F32),
            pltpu.VMEM((2, rank // 4, rank // 4), F32),
            pltpu.VMEM((2, rank // 4, rank // 2), F32),
            pltpu.VMEM((2, rank // 2, rank // 2), F32),
            pltpu.VMEM((rank // 2, rank // 2), F32),
            pltpu.VMEM((rank, rank), F32),
            pltpu.VMEM((rank, rank), F32),
            pltpu.VMEM((rank, width), F32),
            pltpu.VMEM((rank, width), F32),
            pltpu.VMEM((rank // groups, width), F32),
            pltpu.SemaphoreType.DMA((4,)),
            pltpu.SemaphoreType.DMA((3,)),
            pltpu.SemaphoreType.DMA((2, 3)),
            pltpu.SemaphoreType.DMA,
            pltpu.SemaphoreType.DMA((2,)),
            pltpu.SemaphoreType.DMA((4,)),
            pltpu.SemaphoreType.DMA((groups,)),
            pltpu.SemaphoreType.DMA,
        ],
        compiler_params=pltpu.CompilerParams(
            collective_id=0, has_side_effects=True, vmem_limit_bytes=63 << 20
        ),
    )(leaf_blocks, leaf_rhs, bases, couplings)


def solution(mesh):
    placed = (
        P("grp", None, None),
        P("grp", None, "blk"),
        P("grp", None, None),
        P("grp", None, None),
    )
    return jax.shard_map(
        body, mesh=mesh, in_specs=placed, out_specs=P("grp", "blk"), check_vma=False
    )
```
